32 devices in a mesh: blk: 16 (over z, x, core), panel: 2 (over y).
Axes of the slice: x: 2, y: 2, z: 4, core: 2. Of those that a mesh axis runs over, the one named last changes fastest.
Arguments:
- tiles: bfloat16 [16384, 2, 8, 256], P('blk', 'panel'), may hold values from -6 to 6
- loadings: float32 [16384, 512], P('blk'), may hold values from -6 to 6
- maps: float32 [16, 2, 256, 512], P('blk', 'panel'), may hold values from -6 to 6
- run_counts: int32 [64], P('blk'), may hold values from 64 to 256, as said below
Outputs:
- loadings_out: float32 [16384, 512], P(('blk', 'panel'))
- maps_after: float32 [16, 2, 256, 512], P('blk', 'panel')
The draws below stay inside these ranges and needn't reach their ends.
Inputs may be any that keep to these rules, and one draw needn't show every extreme that they name: `run_counts`: valid frames at the start of each run of 256 frames; some run has all 256 valid and some only 64.
All inputs are finite; a program needn't handle non-finite values.
Results may differ from the reference program's by a relative error of at most 0.0028.
Values may be sent and summed in bfloat16 or wider, within the bound.
A program may use at most 64 MiB of HBM per device.

```python
import jax
import jax.numpy as jnp
from jax import lax

R = 512
G = 256
RUN_LEN = 256
RUNS_DEV = 4
STEPS = 8
FRAMES_DEV = 1024
FRAMES = 16384
N_BLK = 16
N_PANEL = 2


def draw_run_counts(key, part):
    total = N_BLK * RUNS_DEV
    first, second, third = jax.random.split(jax.random.fold_in(key, 17), 3)
    values = jax.random.randint(first, (total,), RUN_LEN // 4, RUN_LEN + 1)
    place = jax.random.randint(second, (), 0, total)
    other = (place + 1 + jax.random.randint(third, (), 0, total - 1)) % total
    values = values.at[place].set(RUN_LEN)
    values = values.at[other].set(RUN_LEN // 4)
    return values.astype(jnp.int32)


def factor_draw(key, rows, width):
    first = jax.random.fold_in(key, 0)
    values = jax.random.normal(first, (rows, width), jnp.float32)
    return jnp.clip(values, -6.0, 6.0)


def draw_loadings(key, part):
    values = factor_draw(jax.random.fold_in(key, 23), FRAMES, R)
    return values.astype(jnp.float32)


def draw_maps(key, part):
    values = factor_draw(jax.random.fold_in(key, 29), N_BLK * N_PANEL * G, R)
    return values.reshape(N_BLK, N_PANEL, G, R).astype(jnp.float32)


def shard_levels(own_key, shape, cuts, least, largest):
    def one(dim, shards_of):
        heights = jax.random.uniform(jax.random.fold_in(jax.random.fold_in(own_key, 6), dim), (shards_of,), jnp.float32, least / len(cuts), largest / len(cuts))
        return jnp.repeat(jnp.exp(heights), shape[dim] // shards_of).reshape((-1,) + (1,) * (len(shape) - dim - 1))

    factor_of = one(*cuts[0])
    for cut in cuts[1:]:
        factor_of = factor_of * one(*cut)
    return factor_of


def bell_draw(rng, shape, spread, most, cuts=(), kind=jnp.bfloat16):
    drawn = spread * jax.random.normal(rng, shape, jnp.float32)
    if cuts:
        drawn = drawn * shard_levels(rng, shape, cuts, -0.22, 0.18)
    return jnp.clip(drawn, -most, most).astype(kind)


def setup_inputs(seed: int = 0) -> dict:
    splits = jax.random.split(jax.random.key(seed), 5)
    return {
        "tiles": bell_draw(splits[0], (FRAMES, N_PANEL, STEPS, G), 1.0, 6.0, ((0, 16), (1, 2))),
        "loadings": draw_loadings(jax.random.fold_in(splits[4], 71), 0),
        "maps": draw_maps(jax.random.fold_in(splits[4], 71), 0),
        "run_counts": draw_run_counts(jax.random.fold_in(splits[4], 71), 0),
    }


map_rate = 0.1
load_rate = 0.05


def reference(tiles, loadings, maps, run_counts):
    scale = 1.0 / (R ** 0.5)
    runs = run_counts.reshape(N_BLK, RUNS_DEV)
    within = jnp.arange(FRAMES_DEV, dtype=jnp.int32)
    limits = jnp.repeat(runs, RUN_LEN, axis=1)
    mask = ((within % RUN_LEN)[None, :] < limits).astype(jnp.float32)
    current = loadings.reshape(N_BLK, FRAMES_DEV, R)
    data = tiles.reshape(N_BLK, FRAMES_DEV, N_PANEL, STEPS, G)
    held = maps
    half = STEPS // 2
    for part in range(2):
        loads_bf = current.astype(jnp.bfloat16)
        acc = jnp.zeros((N_BLK, FRAMES_DEV, R), jnp.float32)
        for step in range(part * half, (part + 1) * half):
            def one(items):
                tile, lb, block, rows = items
                xs = tile[:, :, step, :].astype(jnp.float32)
                bb = block.astype(jnp.bfloat16).astype(jnp.float32)
                lf = lb.astype(jnp.float32)
                prod = jnp.einsum('fr,pgr->fpg', lf, bb)
                resid = ((xs - prod * scale) * rows[:, None, None]).astype(jnp.bfloat16).astype(jnp.float32)
                grad_map = jnp.einsum('fpg,fr->pgr', resid, lf) * scale
                grad_load = jnp.einsum('fpg,pgr->fr', resid, bb) * scale
                return block + map_rate * grad_map, grad_load
            held, grads = lax.map(one, (data, loads_bf, held, mask))
            acc = acc + grads
            held = jnp.roll(held, 1, axis=0)
        current = current + load_rate * acc
    return current.reshape(FRAMES, R), held
```

```python
import functools

import jax
import jax.numpy as jnp
from jax import lax
from jax.experimental import pallas as pl
from jax.experimental.pallas import tpu as pltpu
from jax.sharding import PartitionSpec as P

RUN_LEN = 256
MESH = pl.DeviceIdType.MESH
LEVELS = 32767.0

map_rate = 0.1
load_rate = 0.05


def dot(a, b):
    return jnp.dot(a, b, preferred_element_type=jnp.float32)


def dot_nt(a, b):
    return lax.dot_general(a, b, (((1,), (1,)), ((), ())), preferred_element_type=jnp.float32)


def kernel(
    n, steps, tiles_ref, loads_ref, maps_ref, counts_ref, rows_out, maps_out,
    data, mask, loads_bf, loads_t, acc, resid, block_t, start_t, cur,
    code_out, code_in, unit_out, unit_in, share_out, share_in,
    code_send, code_recv, unit_send, unit_recv, share_send, share_recv, new_send, new_recv,
):
    frames, rank = loads_ref.shape
    grays = maps_ref.shape[0]
    lanes = 128
    chunks = grays // lanes
    half_rows = frames // 2
    half = steps // 2
    scale = 1.0 / rank**0.5
    pieces = share_send.shape[1]
    piece = half_rows // pieces
    me = lax.axis_index("blk")
    panel = lax.axis_index("panel")
    right, left = lax.rem(me + 1, n), lax.rem(me + n - 1, n)
    other = 1 - panel

    barrier = pltpu.get_barrier_semaphore()
    for target in ((left, panel), (right, panel), (me, other)):
        pl.semaphore_signal(barrier, inc=1, device_id=target, device_id_type=MESH)

    def code_copy(step, c):
        return pltpu.make_async_remote_copy(
            src_ref=code_out.at[step, c], dst_ref=code_in.at[step, c],
            send_sem=code_send.at[step, c], recv_sem=code_recv.at[step, c],
            device_id=(right, panel), device_id_type=MESH)

    def unit_copy(step, c):
        return pltpu.make_async_remote_copy(
            src_ref=unit_out.at[step, c], dst_ref=unit_in.at[step, c],
            send_sem=unit_send.at[step, c], recv_sem=unit_recv.at[step, c],
            device_id=(right, panel), device_id_type=MESH)

    def share_copy(part, k):
        return pltpu.make_async_remote_copy(
            src_ref=share_out.at[part, k], dst_ref=share_in.at[part, k],
            send_sem=share_send.at[part, k], recv_sem=share_recv.at[part, k],
            device_id=(me, other), device_id_type=MESH)

    def rows_of(owner, k):
        return pl.ds(pl.multiple_of(owner * half_rows + k * piece, piece), piece)

    def new_copy(owner, k):
        rows = rows_of(owner, k)
        return pltpu.make_async_remote_copy(
            src_ref=loads_bf.at[1, rows], dst_ref=loads_bf.at[1, rows],
            send_sem=new_send.at[k], recv_sem=new_recv.at[k],
            device_id=(me, other), device_id_type=MESH)

    for r in range(0, frames, RUN_LEN):
        part_bf = loads_ref[r : r + RUN_LEN, :].astype(jnp.bfloat16)
        loads_bf[0, r : r + RUN_LEN, :] = part_bf
        loads_t[:, r : r + RUN_LEN] = part_bf.T
        within = lax.broadcasted_iota(jnp.int32, (RUN_LEN, lanes), 0)
        mask[r : r + RUN_LEN, :] = (within < counts_ref[r // RUN_LEN]).astype(jnp.float32)
    start_t[...] = maps_ref[...].T

    group = 256
    each = group // steps
    to = lax.broadcasted_iota(jnp.int32, (group, group), 0)
    frm = lax.broadcasted_iota(jnp.int32, (group, group), 1)
    order = jnp.where(frm == lax.rem(to, each) * steps + to // each, 1.0, 0.0).astype(jnp.bfloat16)

    def sort_rows(i, carry):
        block = tiles_ref[pl.ds(pl.multiple_of(i * group, group), group), :]
        sorted_rows = dot(order, block).astype(jnp.bfloat16)
        for s in range(steps):
            data[s, pl.ds(pl.multiple_of(i * each, each), each), :] = (
                sorted_rows[s * each : (s + 1) * each, :])
        return carry

    lax.fori_loop(0, frames * steps // group, sort_rows, 0)
    pl.semaphore_wait(barrier, 3)

    def decoded(step, c):
        return code_in[step, c].astype(jnp.float32) * unit_in[step, c][0:1, :]

    def run_step(step, part, first):
        for c in range(chunks):
            cols = slice(c * lanes, (c + 1) * lanes)
            if first:
                held = start_t[:, cols]
            else:
                code_copy(step - 1, c).wait_recv()
                unit_copy(step - 1, c).wait_recv()
                held = decoded(step - 1, c)
            block = held.astype(jnp.bfloat16)
            block_t[:, cols] = block
            for r in range(0, frames, RUN_LEN):
                rows = slice(r, r + RUN_LEN)
                prod = dot(loads_bf[part, rows, :], block)
                tile = data[step, rows, cols].astype(jnp.float32)
                resid[rows, cols] = ((tile - prod * scale) * mask[rows, :]).astype(jnp.bfloat16)
            new = held + (map_rate * scale) * dot(loads_t[...], resid[:, cols])
            top = jnp.maximum(jnp.max(jnp.abs(new), axis=0, keepdims=True), 1e-30)
            code_out[step, c] = jnp.round(new * (LEVELS / top)).astype(jnp.int32).astype(jnp.int16)
            unit_out[step, c] = jnp.broadcast_to(top * (1.0 / LEVELS), (8, lanes))
            unit_copy(step, c).start()
            code_copy(step, c).start()
        for r in range(0, frames, RUN_LEN):
            rows = slice(r, r + RUN_LEN)
            grad = dot_nt(resid[rows, :], block_t[...])
            acc[rows, :] = grad if first else acc[rows, :] + grad

    def send_shares(part):
        for k in range(pieces):
            share_out[part, k] = acc[rows_of(other, k), :].astype(jnp.bfloat16)
            share_copy(part, k).start()

    def total_of(part, k):
        share_copy(part, k).wait_recv()
        total = acc[rows_of(panel, k), :] + share_in[part, k].astype(jnp.float32)
        return total * (load_rate * scale)

    run_step(0, 0, True)

    def first_half(step, carry):
        run_step(step, 0, False)
        return carry

    lax.fori_loop(1, half, first_half, 0)

    send_shares(0)
    for k in range(pieces):
        rows = rows_of(panel, k)
        own = loads_ref[rows, :] + total_of(0, k)
        cur[k] = own
        own_bf = own.astype(jnp.bfloat16)
        loads_bf[1, rows, :] = own_bf
        new_copy(panel, k).start()
        loads_t[:, rows] = own_bf.T
    acc[...] = jnp.zeros_like(acc)
    for k in range(pieces):
        new_copy(other, k).wait_recv()
        rows = rows_of(other, k)
        loads_t[:, rows] = loads_bf[1, rows, :].T

    def second_half(step, carry):
        run_step(step, 1, False)
        return carry

    lax.fori_loop(half, steps, second_half, 0)

    send_shares(1)
    for c in range(chunks):
        code_copy(steps - 1, c).wait_recv()
        unit_copy(steps - 1, c).wait_recv()
        maps_out[c * lanes : (c + 1) * lanes, :] = decoded(steps - 1, c).T
    for k in range(pieces):
        rows_out[k * piece : (k + 1) * piece, :] = cur[k] + total_of(1, k)

    for k in range(pieces):
        new_copy(panel, k).wait_send()
        for part in range(2):
            share_copy(part, k).wait_send()

    def drain(step, carry):
        for c in range(chunks):
            code_copy(step, c).wait_send()
            unit_copy(step, c).wait_send()
        return carry

    lax.fori_loop(0, steps, drain, 0)


def per_device(n, tiles, loadings, maps, run_counts):
    frames, _, steps, grays = tiles.shape
    rank = maps.shape[-1]
    lanes, pieces = 128, 4
    chunks = grays // lanes
    half_rows = frames // 2
    piece = half_rows // pieces
    f32, bf16 = jnp.float32, jnp.bfloat16
    vmem = pl.BlockSpec(memory_space=pltpu.VMEM)
    dma = pltpu.SemaphoreType.DMA
    rows_out, maps_out = pl.pallas_call(
        functools.partial(kernel, n, steps),
        out_shape=(
            jax.ShapeDtypeStruct((half_rows, rank), f32),
            jax.ShapeDtypeStruct((grays, rank), f32),
        ),
        in_specs=[vmem, vmem, vmem, pl.BlockSpec(memory_space=pltpu.SMEM)],
        out_specs=(vmem, vmem),
        scratch_shapes=[
            pltpu.VMEM((steps, frames, grays), bf16),
            pltpu.VMEM((frames, lanes), f32),
            pltpu.VMEM((2, frames, rank), bf16),
            pltpu.VMEM((rank, frames), bf16),
            pltpu.VMEM((frames, rank), f32),
            pltpu.VMEM((frames, grays), bf16),
            pltpu.VMEM((rank, grays), bf16),
            pltpu.VMEM((rank, grays), f32),
            pltpu.VMEM((pieces, piece, rank), f32),
            pltpu.VMEM((steps, chunks, rank, lanes), jnp.int16),
            pltpu.VMEM((steps, chunks, rank, lanes), jnp.int16),
            pltpu.VMEM((steps, chunks, 8, lanes), f32),
            pltpu.VMEM((steps, chunks, 8, lanes), f32),
            pltpu.VMEM((2, pieces, piece, rank), bf16),
            pltpu.VMEM((2, pieces, piece, rank), bf16),
            dma((steps, chunks)),
            dma((steps, chunks)),
            dma((steps, chunks)),
            dma((steps, chunks)),
            dma((2, pieces)),
            dma((2, pieces)),
            dma((pieces,)),
            dma((pieces,)),
        ],
        compiler_params=pltpu.CompilerParams(
            collective_id=0, has_side_effects=True, vmem_limit_bytes=56 * 1024 * 1024
        ),
    )(tiles.reshape(frames * steps, grays), loadings, maps[0, 0], run_counts)
    return rows_out, maps_out.reshape(maps.shape)


def solution(mesh):
    in_specs = (
        P("blk", "panel", None, None),
        P("blk", None),
        P("blk", "panel", None, None),
        P("blk"),
    )
    out_specs = (P(("blk", "panel"), None), P("blk", "panel", None, None))
    return jax.shard_map(
        functools.partial(per_device, mesh.shape["blk"]),
        mesh=mesh, in_specs=in_specs, out_specs=out_specs, check_vma=False,
    )
```

```python
import functools

import jax
import jax.numpy as jnp
from jax import lax
from jax.experimental import pallas as pl
from jax.experimental.pallas import tpu as pltpu
from jax.sharding import PartitionSpec as P

RUN_LEN = 256
MESH = pl.DeviceIdType.MESH
LEVELS = 32767.0

map_rate = 0.1
load_rate = 0.05


def dot(a, b):
    return jnp.dot(a, b, preferred_element_type=jnp.float32)


def dot_nt(a, b):
    return lax.dot_general(a, b, (((1,), (1,)), ((), ())), preferred_element_type=jnp.float32)


def kernel(
    n, steps, tiles_hbm, loads_ref, maps_ref, counts_ref, rows_out, maps_out,
    tiles_ref, tiles_sem, data, mask, loads_bf, loads_t, acc, resid, block_t, start_t, cur,
    code_out, code_in, unit_out, unit_in, share_out, share_in,
    code_send, code_recv, unit_send, unit_recv, share_send, share_recv, new_send, new_recv,
):
    frames, rank = loads_ref.shape
    fetches = tiles_sem.shape[0]

    def fetch(k):
        count = tiles_ref.shape[0] // fetches
        rows = pl.ds(k * count, count)
        return pltpu.make_async_copy(tiles_hbm.at[rows], tiles_ref.at[rows], tiles_sem.at[k])

    for k in range(fetches):
        fetch(k).start()
    grays = maps_ref.shape[0]
    lanes = 128
    chunks = grays // lanes
    half_rows = frames // 2
    half = steps // 2
    scale = 1.0 / rank**0.5
    pieces = share_send.shape[1]
    piece = half_rows // pieces
    me = lax.axis_index("blk")
    panel = lax.axis_index("panel")
    right, left = lax.rem(me + 1, n), lax.rem(me + n - 1, n)
    other = 1 - panel

    barrier = pltpu.get_barrier_semaphore()
    for target in ((left, panel), (right, panel), (me, other)):
        pl.semaphore_signal(barrier, inc=1, device_id=target, device_id_type=MESH)

    def code_copy(step, c):
        return pltpu.make_async_remote_copy(
            src_ref=code_out.at[step, c], dst_ref=code_in.at[step, c],
            send_sem=code_send.at[step, c], recv_sem=code_recv.at[step, c],
            device_id=(right, panel), device_id_type=MESH)

    def unit_copy(step, c):
        return pltpu.make_async_remote_copy(
            src_ref=unit_out.at[step, c], dst_ref=unit_in.at[step, c],
            send_sem=unit_send.at[step, c], recv_sem=unit_recv.at[step, c],
            device_id=(right, panel), device_id_type=MESH)

    def share_copy(part, k):
        return pltpu.make_async_remote_copy(
            src_ref=share_out.at[part, k], dst_ref=share_in.at[part, k],
            send_sem=share_send.at[part, k], recv_sem=share_recv.at[part, k],
            device_id=(me, other), device_id_type=MESH)

    def rows_of(owner, k):
        return pl.ds(pl.multiple_of(owner * half_rows + k * piece, piece), piece)

    def new_copy(owner, k):
        rows = rows_of(owner, k)
        return pltpu.make_async_remote_copy(
            src_ref=loads_bf.at[1, rows], dst_ref=loads_bf.at[1, rows],
            send_sem=new_send.at[k], recv_sem=new_recv.at[k],
            device_id=(me, other), device_id_type=MESH)

    for r in range(0, frames, RUN_LEN):
        part_bf = loads_ref[r : r + RUN_LEN, :].astype(jnp.bfloat16)
        loads_bf[0, r : r + RUN_LEN, :] = part_bf
        loads_t[:, r : r + RUN_LEN] = part_bf.T
        within = lax.broadcasted_iota(jnp.int32, (RUN_LEN, lanes), 0)
        mask[r : r + RUN_LEN, :] = (within < counts_ref[r // RUN_LEN]).astype(jnp.float32)
    start_t[...] = maps_ref[...].T

    group = 256
    each = group // steps
    to = lax.broadcasted_iota(jnp.int32, (group, group), 0)
    frm = lax.broadcasted_iota(jnp.int32, (group, group), 1)
    order = jnp.where(frm == lax.rem(to, each) * steps + to // each, 1.0, 0.0).astype(jnp.bfloat16)

    blocks = frames * steps // group
    for k in range(fetches):
        fetch(k).wait()

        def sort_rows(i, carry):
            for j in range(blocks // fetches // 2):
                at = i * (blocks // fetches // 2) + j
                block = tiles_ref[pl.ds(pl.multiple_of(at * group, group), group), :]
                sorted_rows = dot(order, block).astype(jnp.bfloat16)
                for s in range(steps):
                    data[s, pl.ds(pl.multiple_of(at * each, each), each), :] = (
                        sorted_rows[s * each : (s + 1) * each, :])
            return carry

        lax.fori_loop(2 * k, 2 * k + 2, sort_rows, 0)
    pl.semaphore_wait(barrier, 3)

    def decoded(step, c):
        return code_in[step, c].astype(jnp.float32) * unit_in[step, c][0:1, :]

    def send_block(step, c, new):
        top = jnp.maximum(jnp.max(jnp.abs(new), axis=0, keepdims=True), 1e-30)
        code_out[step, c] = jnp.round(new * (LEVELS / top)).astype(jnp.int32).astype(jnp.int16)
        unit_out[step, c] = jnp.broadcast_to(top * (1.0 / LEVELS), (8, lanes))
        unit_copy(step, c).start()
        code_copy(step, c).start()

    def run_step(step, part, first):
        for c in range(chunks):
            cols = slice(c * lanes, (c + 1) * lanes)
            if first:
                held = start_t[:, cols]
            else:
                code_copy(step - 1, c).wait_recv()
                unit_copy(step - 1, c).wait_recv()
                held = decoded(step - 1, c)
            block = held.astype(jnp.bfloat16)
            block_t[:, cols] = block
            for r in range(0, frames, RUN_LEN):
                rows = slice(r, r + RUN_LEN)
                prod = dot(loads_bf[part, rows, :], block)
                tile = data[step, rows, cols].astype(jnp.float32)
                resid[rows, cols] = ((tile - prod * scale) * mask[rows, :]).astype(jnp.bfloat16)
            new = held + (map_rate * scale) * dot(loads_t[...], resid[:, cols])
            send_block(step, c, new)
        for r in range(0, frames, RUN_LEN):
            rows = slice(r, r + RUN_LEN)
            grad = dot_nt(resid[rows, :], block_t[...])
            acc[rows, :] = grad if first else acc[rows, :] + grad
    def send_shares(part):
        for k in range(pieces):
            share_out[part, k] = acc[rows_of(other, k), :].astype(jnp.bfloat16)
            share_copy(part, k).start()

    def total_of(part, k):
        share_copy(part, k).wait_recv()
        total = acc[rows_of(panel, k), :] + share_in[part, k].astype(jnp.float32)
        return total * (load_rate * scale)

    run_step(0, 0, True)

    def first_half(step, carry):
        run_step(step, 0, False)
        return carry

    lax.fori_loop(1, half, first_half, 0)

    send_shares(0)
    for c in range(chunks):
        cols = slice(c * lanes, (c + 1) * lanes)
        code_copy(half - 1, c).wait_recv()
        unit_copy(half - 1, c).wait_recv()
        held = decoded(half - 1, c)
        start_t[:, cols] = held
        block_t[:, cols] = held.astype(jnp.bfloat16)

    def run_piece(rows):
        rows_bf = loads_bf[1, rows, :]
        rows_t = rows_bf.T
        loads_t[:, rows] = rows_t
        prod = dot(rows_bf, block_t[...])
        for c in range(chunks):
            cols = slice(c * lanes, (c + 1) * lanes)
            tile = data[half, rows, cols].astype(jnp.float32)
            resid[rows, cols] = ((tile - prod[:, cols] * scale) * mask[rows, :]).astype(jnp.bfloat16)
        part_resid = resid[rows, :]
        start_t[...] += (map_rate * scale) * dot(rows_t, part_resid)
        acc[rows, :] = dot_nt(part_resid, block_t[...])

    for k in range(pieces):
        rows = rows_of(panel, k)
        own = loads_ref[rows, :] + total_of(0, k)
        cur[k] = own
        loads_bf[1, rows, :] = own.astype(jnp.bfloat16)
        new_copy(panel, k).start()
        run_piece(rows)
    for k in range(pieces):
        new_copy(other, k).wait_recv()
        run_piece(rows_of(other, k))
    for c in range(chunks):
        send_block(half, c, start_t[:, c * lanes : (c + 1) * lanes])

    def second_half(step, carry):
        run_step(step, 1, False)
        return carry

    lax.fori_loop(half + 1, steps, second_half, 0)

    send_shares(1)
    for c in range(chunks):
        code_copy(steps - 1, c).wait_recv()
        unit_copy(steps - 1, c).wait_recv()
        maps_out[c * lanes : (c + 1) * lanes, :] = decoded(steps - 1, c).T
    for k in range(pieces):
        rows_out[k * piece : (k + 1) * piece, :] = cur[k] + total_of(1, k)

    for k in range(pieces):
        new_copy(panel, k).wait_send()
        for part in range(2):
            share_copy(part, k).wait_send()

    def drain(step, carry):
        for c in range(chunks):
            code_copy(step, c).wait_send()
            unit_copy(step, c).wait_send()
        return carry

    lax.fori_loop(0, steps, drain, 0)


def finish(rows_in, maps_in, rows_out, maps_out):
    rows_out[...] = rows_in[...]
    maps_out[...] = maps_in[...]


def per_device(n, tiles, loadings, maps, run_counts):
    frames, _, steps, grays = tiles.shape
    rank = maps.shape[-1]
    lanes, pieces = 128, 4
    chunks = grays // lanes
    half_rows = frames // 2
    piece = half_rows // pieces
    f32, bf16 = jnp.float32, jnp.bfloat16
    vmem = pl.BlockSpec(memory_space=pltpu.VMEM)
    anywhere = pl.BlockSpec(memory_space=pl.ANY)
    fetches = 4
    dma = pltpu.SemaphoreType.DMA
    rows_out, maps_out = pl.pallas_call(
        functools.partial(kernel, n, steps),
        out_shape=(
            jax.ShapeDtypeStruct((half_rows, rank), f32),
            jax.ShapeDtypeStruct((grays, rank), f32),
        ),
        in_specs=[anywhere, vmem, vmem, pl.BlockSpec(memory_space=pltpu.SMEM)],
        out_specs=(vmem, vmem),
        scratch_shapes=[
            pltpu.VMEM((frames * steps, grays), bf16),
            dma((fetches,)),
            pltpu.VMEM((steps, frames, grays), bf16),
            pltpu.VMEM((frames, lanes), f32),
            pltpu.VMEM((2, frames, rank), bf16),
            pltpu.VMEM((rank, frames), bf16),
            pltpu.VMEM((frames, rank), f32),
            pltpu.VMEM((frames, grays), bf16),
            pltpu.VMEM((rank, grays), bf16),
            pltpu.VMEM((rank, grays), f32),
            pltpu.VMEM((pieces, piece, rank), f32),
            pltpu.VMEM((steps, chunks, rank, lanes), jnp.int16),
            pltpu.VMEM((steps, chunks, rank, lanes), jnp.int16),
            pltpu.VMEM((steps, chunks, 8, lanes), f32),
            pltpu.VMEM((steps, chunks, 8, lanes), f32),
            pltpu.VMEM((2, pieces, piece, rank), bf16),
            pltpu.VMEM((2, pieces, piece, rank), bf16),
            dma((steps, chunks)),
            dma((steps, chunks)),
            dma((steps, chunks)),
            dma((steps, chunks)),
            dma((2, pieces)),
            dma((2, pieces)),
            dma((pieces,)),
            dma((pieces,)),
        ],
        compiler_params=pltpu.CompilerParams(
            collective_id=0, has_side_effects=True, vmem_limit_bytes=48 * 1024 * 1024
        ),
    )(tiles.reshape(frames * steps, grays), loadings, maps[0, 0], run_counts)
    rows_out, maps_out = pl.pallas_call(
        finish,
        out_shape=(
            jax.ShapeDtypeStruct(rows_out.shape, f32),
            jax.ShapeDtypeStruct(maps_out.shape, f32),
        ),
        in_specs=[vmem, vmem],
        out_specs=(vmem, vmem),
    )(rows_out, maps_out)
    return rows_out, maps_out.reshape(maps.shape)


def solution(mesh):
    in_specs = (
        P("blk", "panel", None, None),
        P("blk", None),
        P("blk", "panel", None, None),
        P("blk"),
    )
    out_specs = (P(("blk", "panel"), None), P("blk", "panel", None, None))
    return jax.shard_map(
        functools.partial(per_device, mesh.shape["blk"]),
        mesh=mesh, in_specs=in_specs, out_specs=out_specs, check_vma=False,
    )
```

```python
import functools

import jax
import jax.numpy as jnp
from jax import lax
from jax.experimental import pallas as pl
from jax.experimental.pallas import tpu as pltpu
from jax.sharding import PartitionSpec as P

RUN_LEN = 256
MESH = pl.DeviceIdType.MESH
LEVELS = 32767.0

map_rate = 0.1
load_rate = 0.05


def dot(a, b):
    return jnp.dot(a, b, preferred_element_type=jnp.float32)


def dot_nt(a, b):
    return lax.dot_general(a, b, (((1,), (1,)), ((), ())), preferred_element_type=jnp.float32)


def kernel(
    n, steps, tiles_hbm, loads_hbm, maps_hbm, counts_ref, rows_out, maps_out,
    tiles_ref, loads_ref, maps_ref, tiles_sem, loads_sem, maps_sem, rows_sem, out_sem, data, mask, loads_bf, loads_t, acc, resid, block_t, start_t, cur,
    code_out, code_in, unit_out, unit_in, share_out, share_in,
    code_send, code_recv, unit_send, unit_recv, share_send, share_recv, new_send, new_recv,
):
    frames, rank = loads_ref.shape
    fetches = tiles_sem.shape[0]

    def fetch(src, dst, sems, k):
        count = dst.shape[0] // fetches
        rows = pl.ds(k * count, count)
        return pltpu.make_async_copy(src.at[rows], dst.at[rows], sems.at[k])

    for k in range(fetches):
        fetch(loads_hbm, loads_ref, loads_sem, k).start()
    fetch_maps = pltpu.make_async_copy(maps_hbm, maps_ref, maps_sem)
    fetch_maps.start()

    for k in range(fetches):
        fetch(tiles_hbm, tiles_ref, tiles_sem, k).start()
    grays = maps_ref.shape[0]
    lanes = 128
    chunks = grays // lanes
    half_rows = frames // 2
    half = steps // 2
    scale = 1.0 / rank**0.5
    pieces = share_send.shape[1]
    piece = half_rows // pieces
    me = lax.axis_index("blk")
    panel = lax.axis_index("panel")
    right, left = lax.rem(me + 1, n), lax.rem(me + n - 1, n)
    other = 1 - panel

    barrier = pltpu.get_barrier_semaphore()
    for target in ((left, panel), (right, panel), (me, other)):
        pl.semaphore_signal(barrier, inc=1, device_id=target, device_id_type=MESH)

    def code_copy(step, c):
        return pltpu.make_async_remote_copy(
            src_ref=code_out.at[step, c], dst_ref=code_in.at[step, c],
            send_sem=code_send.at[step, c], recv_sem=code_recv.at[step, c],
            device_id=(right, panel), device_id_type=MESH)

    def unit_copy(step, c):
        return pltpu.make_async_remote_copy(
            src_ref=unit_out.at[step, c], dst_ref=unit_in.at[step, c],
            send_sem=unit_send.at[step, c], recv_sem=unit_recv.at[step, c],
            device_id=(right, panel), device_id_type=MESH)

    def share_copy(part, k):
        return pltpu.make_async_remote_copy(
            src_ref=share_out.at[part, k], dst_ref=share_in.at[part, k],
            send_sem=share_send.at[part, k], recv_sem=share_recv.at[part, k],
            device_id=(me, other), device_id_type=MESH)

    def rows_of(owner, k):
        return pl.ds(pl.multiple_of(owner * half_rows + k * piece, piece), piece)

    def new_copy(owner, k):
        rows = rows_of(owner, k)
        return pltpu.make_async_remote_copy(
            src_ref=loads_bf.at[1, rows], dst_ref=loads_bf.at[1, rows],
            send_sem=new_send.at[k], recv_sem=new_recv.at[k],
            device_id=(me, other), device_id_type=MESH)

    for r in range(0, frames, RUN_LEN):
        if r % (frames // fetches) == 0:
            fetch(loads_hbm, loads_ref, loads_sem, r // (frames // fetches)).wait()
        part_bf = loads_ref[r : r + RUN_LEN, :].astype(jnp.bfloat16)
        loads_bf[0, r : r + RUN_LEN, :] = part_bf
        loads_t[:, r : r + RUN_LEN] = part_bf.T
        within = lax.broadcasted_iota(jnp.int32, (RUN_LEN, lanes), 0)
        mask[r : r + RUN_LEN, :] = (within < counts_ref[r // RUN_LEN]).astype(jnp.float32)
    fetch_maps.wait()
    start_t[...] = maps_ref[...].T

    group = 256
    each = group // steps
    to = lax.broadcasted_iota(jnp.int32, (group, group), 0)
    frm = lax.broadcasted_iota(jnp.int32, (group, group), 1)
    order = jnp.where(frm == lax.rem(to, each) * steps + to // each, 1.0, 0.0).astype(jnp.bfloat16)

    blocks = frames * steps // group
    for k in range(fetches):
        fetch(tiles_hbm, tiles_ref, tiles_sem, k).wait()

        def sort_rows(i, carry):
            for j in range(blocks // fetches // 2):
                at = i * (blocks // fetches // 2) + j
                block = tiles_ref[pl.ds(pl.multiple_of(at * group, group), group), :]
                sorted_rows = dot(order, block).astype(jnp.bfloat16)
                for s in range(steps):
                    data[s, pl.ds(pl.multiple_of(at * each, each), each), :] = (
                        sorted_rows[s * each : (s + 1) * each, :])
            return carry

        lax.fori_loop(2 * k, 2 * k + 2, sort_rows, 0)
    pl.semaphore_wait(barrier, 3)

    def decoded(step, c):
        return code_in[step, c].astype(jnp.float32) * unit_in[step, c][0:1, :]

    def send_block(step, c, new):
        top = jnp.maximum(jnp.max(jnp.abs(new), axis=0, keepdims=True), 1e-30)
        code_out[step, c] = jnp.round(new * (LEVELS / top)).astype(jnp.int32).astype(jnp.int16)
        unit_out[step, c] = jnp.broadcast_to(top * (1.0 / LEVELS), (8, lanes))
        unit_copy(step, c).start()
        code_copy(step, c).start()

    def run_step(step, part, first=False, last=False):
        for c in range(chunks):
            cols = slice(c * lanes, (c + 1) * lanes)
            if first:
                held = start_t[:, cols]
            else:
                code_copy(step - 1, c).wait_recv()
                unit_copy(step - 1, c).wait_recv()
                held = decoded(step - 1, c)
            block = held.astype(jnp.bfloat16)
            block_t[:, cols] = block
            for r in range(0, frames, RUN_LEN):
                rows = slice(r, r + RUN_LEN)
                prod = dot(loads_bf[part, rows, :], block)
                tile = data[step, rows, cols].astype(jnp.float32)
                resid[rows, cols] = ((tile - prod * scale) * mask[rows, :]).astype(jnp.bfloat16)
            new = held + (map_rate * scale) * dot(loads_t[...], resid[:, cols])
            send_block(step, c, new)
        if last:
            for k in range(pieces):
                rows = rows_of(other, k)
                total = acc[rows, :] + dot_nt(resid[rows, :], block_t[...])
                share_out[part, k] = total.astype(jnp.bfloat16)
                share_copy(part, k).start()
            rows = pl.ds(pl.multiple_of(panel * half_rows, half_rows), half_rows)
            acc[rows, :] += dot_nt(resid[rows, :], block_t[...])
        else:
            for r in range(0, frames, RUN_LEN):
                rows = slice(r, r + RUN_LEN)
                grad = dot_nt(resid[rows, :], block_t[...])
                acc[rows, :] = grad if first else acc[rows, :] + grad
    def write_maps(c):
        rows = pl.ds(c * lanes, lanes)
        return pltpu.make_async_copy(maps_ref.at[rows], maps_out.at[rows], out_sem.at[c])

    def write_rows(k):
        return pltpu.make_async_copy(cur.at[k], rows_out.at[pl.ds(k * piece, piece)], rows_sem.at[k])

    def total_of(part, k):
        share_copy(part, k).wait_recv()
        total = acc[rows_of(panel, k), :] + share_in[part, k].astype(jnp.float32)
        return total * (load_rate * scale)

    run_step(0, 0, first=True)

    def first_half(step, carry):
        run_step(step, 0)
        return carry

    lax.fori_loop(1, half - 1, first_half, 0)
    run_step(half - 1, 0, last=True)

    for c in range(chunks):
        cols = slice(c * lanes, (c + 1) * lanes)
        code_copy(half - 1, c).wait_recv()
        unit_copy(half - 1, c).wait_recv()
        held = decoded(half - 1, c)
        start_t[:, cols] = held
        block_t[:, cols] = held.astype(jnp.bfloat16)

    def run_piece(rows):
        rows_bf = loads_bf[1, rows, :]
        rows_t = rows_bf.T
        loads_t[:, rows] = rows_t
        prod = dot(rows_bf, block_t[...])
        for c in range(chunks):
            cols = slice(c * lanes, (c + 1) * lanes)
            tile = data[half, rows, cols].astype(jnp.float32)
            resid[rows, cols] = ((tile - prod[:, cols] * scale) * mask[rows, :]).astype(jnp.bfloat16)
        part_resid = resid[rows, :]
        start_t[...] += (map_rate * scale) * dot(rows_t, part_resid)
        acc[rows, :] = dot_nt(part_resid, block_t[...])

    for k in range(pieces):
        rows = rows_of(panel, k)
        own = loads_ref[rows, :] + total_of(0, k)
        cur[k] = own
        loads_bf[1, rows, :] = own.astype(jnp.bfloat16)
        new_copy(panel, k).start()
        run_piece(rows)
    for k in range(pieces):
        new_copy(other, k).wait_recv()
        run_piece(rows_of(other, k))
    for c in range(chunks):
        send_block(half, c, start_t[:, c * lanes : (c + 1) * lanes])

    def second_half(step, carry):
        run_step(step, 1)
        return carry

    lax.fori_loop(half + 1, steps - 1, second_half, 0)
    run_step(steps - 1, 1, last=True)

    for c in range(chunks):
        code_copy(steps - 1, c).wait_recv()
        unit_copy(steps - 1, c).wait_recv()
        maps_ref[c * lanes : (c + 1) * lanes, :] = decoded(steps - 1, c).T
        write_maps(c).start()
    for k in range(pieces):
        cur[k] = cur[k] + total_of(1, k)
        write_rows(k).start()
    for c in range(chunks):
        write_maps(c).wait()
    for k in range(pieces):
        write_rows(k).wait()

    for k in range(pieces):
        new_copy(panel, k).wait_send()
        for part in range(2):
            share_copy(part, k).wait_send()

    def drain(step, carry):
        for c in range(chunks):
            code_copy(step, c).wait_send()
            unit_copy(step, c).wait_send()
        return carry

    lax.fori_loop(0, steps, drain, 0)


def finish(rows_in, maps_in, rows_out, maps_out, sems):
    copies = []
    for src, dst in ((rows_in, rows_out), (maps_in, maps_out)):
        count = src.shape[0] // 4
        for k in range(4):
            rows = pl.ds(k * count, count)
            copies.append(pltpu.make_async_copy(src.at[rows], dst.at[rows], sems.at[len(copies)]))
    for copy in copies:
        copy.start()
    for copy in copies:
        copy.wait()


def per_device(n, tiles, loadings, maps, run_counts):
    frames, _, steps, grays = tiles.shape
    rank = maps.shape[-1]
    lanes, pieces = 128, 4
    chunks = grays // lanes
    half_rows = frames // 2
    piece = half_rows // pieces
    f32, bf16 = jnp.float32, jnp.bfloat16
    anywhere = pl.BlockSpec(memory_space=pl.ANY)
    fetches = 4
    dma = pltpu.SemaphoreType.DMA
    rows_out, maps_out = pl.pallas_call(
        functools.partial(kernel, n, steps),
        out_shape=(
            jax.ShapeDtypeStruct((half_rows, rank), f32),
            jax.ShapeDtypeStruct((grays, rank), f32),
        ),
        in_specs=[anywhere, anywhere, anywhere, pl.BlockSpec(memory_space=pltpu.SMEM)],
        out_specs=(anywhere, anywhere),
        scratch_shapes=[
            pltpu.VMEM((frames * steps, grays), bf16),
            pltpu.VMEM((frames, rank), f32),
            pltpu.VMEM((grays, rank), f32),
            dma((fetches,)),
            dma((fetches,)),
            dma(()),
            dma((pieces,)),
            dma((chunks,)),
            pltpu.VMEM((steps, frames, grays), bf16),
            pltpu.VMEM((frames, lanes), f32),
            pltpu.VMEM((2, frames, rank), bf16),
            pltpu.VMEM((rank, frames), bf16),
            pltpu.VMEM((frames, rank), f32),
            pltpu.VMEM((frames, grays), bf16),
            pltpu.VMEM((rank, grays), bf16),
            pltpu.VMEM((rank, grays), f32),
            pltpu.VMEM((pieces, piece, rank), f32),
            pltpu.VMEM((steps, chunks, rank, lanes), jnp.int16),
            pltpu.VMEM((steps, chunks, rank, lanes), jnp.int16),
            pltpu.VMEM((steps, chunks, 8, lanes), f32),
            pltpu.VMEM((steps, chunks, 8, lanes), f32),
            pltpu.VMEM((2, pieces, piece, rank), bf16),
            pltpu.VMEM((2, pieces, piece, rank), bf16),
            dma((steps, chunks)),
            dma((steps, chunks)),
            dma((steps, chunks)),
            dma((steps, chunks)),
            dma((2, pieces)),
            dma((2, pieces)),
            dma((pieces,)),
            dma((pieces,)),
        ],
        compiler_params=pltpu.CompilerParams(
            collective_id=0, has_side_effects=True, vmem_limit_bytes=56 * 1024 * 1024
        ),
    )(tiles.reshape(frames * steps, grays), loadings, maps[0, 0], run_counts)
    rows_out, maps_out = pl.pallas_call(
        finish,
        out_shape=(
            jax.ShapeDtypeStruct(rows_out.shape, f32),
            jax.ShapeDtypeStruct(maps_out.shape, f32),
        ),
        in_specs=[anywhere, anywhere],
        out_specs=(anywhere, anywhere),
        scratch_shapes=[dma((8,))],
        compiler_params=pltpu.CompilerParams(vmem_limit_bytes=56 * 1024 * 1024),
    )(rows_out, maps_out)
    return rows_out, maps_out.reshape(maps.shape)


def solution(mesh):
    in_specs = (
        P("blk", "panel", None, None),
        P("blk", None),
        P("blk", "panel", None, None),
        P("blk"),
    )
    out_specs = (P(("blk", "panel"), None), P("blk", "panel", None, None))
    return jax.shard_map(
        functools.partial(per_device, mesh.shape["blk"]),
        mesh=mesh, in_specs=in_specs, out_specs=out_specs, check_vma=False,
    )
```

```python
import functools

import jax
import jax.numpy as jnp
from jax import lax
from jax.experimental import pallas as pl
from jax.experimental.pallas import tpu as pltpu
from jax.sharding import PartitionSpec as P

RUN_LEN = 256
MESH = pl.DeviceIdType.MESH
LEVELS = 32767.0

map_rate = 0.1
load_rate = 0.05


def dot(a, b):
    return jnp.dot(a, b, preferred_element_type=jnp.float32)


def dot_nt(a, b):
    return lax.dot_general(a, b, (((1,), (1,)), ((), ())), preferred_element_type=jnp.float32)


def kernel(
    n, steps, tiles_hbm, loads_hbm, maps_hbm, counts_ref, rows_out, maps_out,
    tiles_ref, loads_ref, maps_ref, tiles_sem, loads_sem, maps_sem, rows_sem, out_sem, data, mask, loads_bf, loads_t, acc, resid, block_t, start_t, cur,
    code_out, code_in, unit_out, unit_in, share_out, share_in,
    code_send, code_recv, unit_send, unit_recv, share_send, share_recv, new_send, new_recv,
):
    frames, rank = loads_ref.shape
    fetches = tiles_sem.shape[0]

    def fetch(src, dst, sems, k):
        count = dst.shape[0] // fetches
        rows = pl.ds(k * count, count)
        return pltpu.make_async_copy(src.at[rows], dst.at[rows], sems.at[k])

    for k in range(fetches):
        fetch(loads_hbm, loads_ref, loads_sem, k).start()
    fetch_maps = pltpu.make_async_copy(maps_hbm, maps_ref, maps_sem)
    fetch_maps.start()

    for k in range(fetches):
        fetch(tiles_hbm, tiles_ref, tiles_sem, k).start()
    grays = maps_ref.shape[0]
    lanes = 128
    chunks = grays // lanes
    half_rows = frames // 2
    half = steps // 2
    scale = 1.0 / rank**0.5
    pieces = share_send.shape[1]
    piece = half_rows // pieces
    me = lax.axis_index("blk")
    panel = lax.axis_index("panel")
    right, left = lax.rem(me + 1, n), lax.rem(me + n - 1, n)
    other = 1 - panel

    barrier = pltpu.get_barrier_semaphore()
    for target in ((left, panel), (right, panel), (me, other)):
        pl.semaphore_signal(barrier, inc=1, device_id=target, device_id_type=MESH)

    def code_copy(step, c):
        return pltpu.make_async_remote_copy(
            src_ref=code_out.at[step, c], dst_ref=code_in.at[step, c],
            send_sem=code_send.at[step, c], recv_sem=code_recv.at[step, c],
            device_id=(right, panel), device_id_type=MESH)

    def unit_copy(step, c):
        return pltpu.make_async_remote_copy(
            src_ref=unit_out.at[step, c], dst_ref=unit_in.at[step, c],
            send_sem=unit_send.at[step, c], recv_sem=unit_recv.at[step, c],
            device_id=(right, panel), device_id_type=MESH)

    def share_copy(part, k):
        return pltpu.make_async_remote_copy(
            src_ref=share_out.at[part, k], dst_ref=share_in.at[part, k],
            send_sem=share_send.at[part, k], recv_sem=share_recv.at[part, k],
            device_id=(me, other), device_id_type=MESH)

    def rows_of(owner, k):
        return pl.ds(pl.multiple_of(owner * half_rows + k * piece, piece), piece)

    def new_copy(owner, k):
        rows = rows_of(owner, k)
        return pltpu.make_async_remote_copy(
            src_ref=loads_bf.at[1, rows], dst_ref=loads_bf.at[1, rows],
            send_sem=new_send.at[k], recv_sem=new_recv.at[k],
            device_id=(me, other), device_id_type=MESH)

    for r in range(0, frames, RUN_LEN):
        if r % (frames // fetches) == 0:
            fetch(loads_hbm, loads_ref, loads_sem, r // (frames // fetches)).wait()
        part_bf = loads_ref[r : r + RUN_LEN, :].astype(jnp.bfloat16)
        loads_bf[0, r : r + RUN_LEN, :] = part_bf
        loads_t[:, r : r + RUN_LEN] = part_bf.T
        within = lax.broadcasted_iota(jnp.int32, (RUN_LEN, lanes), 0)
        mask[r : r + RUN_LEN, :] = (within < counts_ref[r // RUN_LEN]).astype(jnp.float32)
    fetch_maps.wait()
    start_t[...] = maps_ref[...].T

    group = 256
    each = group // steps
    to = lax.broadcasted_iota(jnp.int32, (group, group), 0)
    frm = lax.broadcasted_iota(jnp.int32, (group, group), 1)
    order = jnp.where(frm == lax.rem(to, each) * steps + to // each, 1.0, 0.0).astype(jnp.bfloat16)

    blocks = frames * steps // group
    per_fetch = blocks // fetches

    def sort_steps(first, stop, per_turn):
        def turn(i, carry):
            for j in range(per_turn):
                at = i * per_turn + j
                block = tiles_ref[pl.ds(pl.multiple_of(at * group, group), group), :]
                sorted_rows = dot(order[first * each : stop * each, :], block).astype(jnp.bfloat16)
                for s in range(first, stop):
                    data[s, pl.ds(pl.multiple_of(at * each, each), each), :] = (
                        sorted_rows[(s - first) * each : (s - first + 1) * each, :])
            return carry

        return turn

    for k in range(fetches):
        fetch(tiles_hbm, tiles_ref, tiles_sem, k).wait()
        sort_steps(0, 1, per_fetch)(k, 0)
    pl.semaphore_wait(barrier, 3)

    def decoded(step, c):
        return code_in[step, c].astype(jnp.float32) * unit_in[step, c][0:1, :]

    def send_block(step, c, new):
        top = jnp.maximum(jnp.max(jnp.abs(new), axis=0, keepdims=True), 1e-30)
        code_out[step, c] = jnp.round(new * (LEVELS / top)).astype(jnp.int32).astype(jnp.int16)
        unit_out[step, c] = jnp.broadcast_to(top * (1.0 / LEVELS), (8, lanes))
        unit_copy(step, c).start()
        code_copy(step, c).start()

    def run_step(step, part, first=False, last=False):
        for c in range(chunks):
            cols = slice(c * lanes, (c + 1) * lanes)
            if first:
                held = start_t[:, cols]
            else:
                code_copy(step - 1, c).wait_recv()
                unit_copy(step - 1, c).wait_recv()
                held = decoded(step - 1, c)
            block = held.astype(jnp.bfloat16)
            block_t[:, cols] = block
            for r in range(0, frames, RUN_LEN):
                rows = slice(r, r + RUN_LEN)
                prod = dot(loads_bf[part, rows, :], block)
                tile = data[step, rows, cols].astype(jnp.float32)
                resid[rows, cols] = ((tile - prod * scale) * mask[rows, :]).astype(jnp.bfloat16)
            new = held + (map_rate * scale) * dot(loads_t[...], resid[:, cols])
            send_block(step, c, new)
        if last:
            for k in range(pieces):
                rows = rows_of(other, k)
                total = acc[rows, :] + dot_nt(resid[rows, :], block_t[...])
                share_out[part, k] = total.astype(jnp.bfloat16)
                share_copy(part, k).start()
            rows = pl.ds(pl.multiple_of(panel * half_rows, half_rows), half_rows)
            acc[rows, :] += dot_nt(resid[rows, :], block_t[...])
        else:
            for r in range(0, frames, RUN_LEN):
                rows = slice(r, r + RUN_LEN)
                grad = dot_nt(resid[rows, :], block_t[...])
                acc[rows, :] = grad if first else acc[rows, :] + grad
    def write_maps(c):
        rows = pl.ds(c * lanes, lanes)
        return pltpu.make_async_copy(maps_ref.at[rows], maps_out.at[rows], out_sem.at[c])

    def write_rows(k):
        return pltpu.make_async_copy(cur.at[k], rows_out.at[pl.ds(k * piece, piece)], rows_sem.at[k])

    def total_of(part, k):
        share_copy(part, k).wait_recv()
        total = acc[rows_of(panel, k), :] + share_in[part, k].astype(jnp.float32)
        return total * (load_rate * scale)

    run_step(0, 0, first=True)
    lax.fori_loop(0, 2 * fetches, sort_steps(1, steps, per_fetch // 2), 0)

    def first_half(step, carry):
        run_step(step, 0)
        return carry

    lax.fori_loop(1, half - 1, first_half, 0)
    run_step(half - 1, 0, last=True)

    for c in range(chunks):
        cols = slice(c * lanes, (c + 1) * lanes)
        code_copy(half - 1, c).wait_recv()
        unit_copy(half - 1, c).wait_recv()
        held = decoded(half - 1, c)
        start_t[:, cols] = held
        block_t[:, cols] = held.astype(jnp.bfloat16)

    def run_piece(rows):
        rows_bf = loads_bf[1, rows, :]
        rows_t = rows_bf.T
        loads_t[:, rows] = rows_t
        prod = dot(rows_bf, block_t[...])
        for c in range(chunks):
            cols = slice(c * lanes, (c + 1) * lanes)
            tile = data[half, rows, cols].astype(jnp.float32)
            resid[rows, cols] = ((tile - prod[:, cols] * scale) * mask[rows, :]).astype(jnp.bfloat16)
        part_resid = resid[rows, :]
        start_t[...] += (map_rate * scale) * dot(rows_t, part_resid)
        acc[rows, :] = dot_nt(part_resid, block_t[...])

    for k in range(pieces):
        rows = rows_of(panel, k)
        own = loads_ref[rows, :] + total_of(0, k)
        cur[k] = own
        loads_bf[1, rows, :] = own.astype(jnp.bfloat16)
        new_copy(panel, k).start()
        run_piece(rows)
    for k in range(pieces):
        new_copy(other, k).wait_recv()
        run_piece(rows_of(other, k))
    for c in range(chunks):
        send_block(half, c, start_t[:, c * lanes : (c + 1) * lanes])

    def second_half(step, carry):
        run_step(step, 1)
        return carry

    lax.fori_loop(half + 1, steps - 1, second_half, 0)
    run_step(steps - 1, 1, last=True)

    for k in range(pieces):
        if k == pieces - 1:
            for c in range(chunks):
                code_copy(steps - 1, c).wait_recv()
                unit_copy(steps - 1, c).wait_recv()
                maps_ref[c * lanes : (c + 1) * lanes, :] = decoded(steps - 1, c).T
                write_maps(c).start()
        cur[k] = cur[k] + total_of(1, k)
        write_rows(k).start()
    for c in range(chunks):
        write_maps(c).wait()
    for k in range(pieces):
        write_rows(k).wait()

    for k in range(pieces):
        new_copy(panel, k).wait_send()
        for part in range(2):
            share_copy(part, k).wait_send()

    def drain(step, carry):
        for c in range(chunks):
            code_copy(step, c).wait_send()
            unit_copy(step, c).wait_send()
        return carry

    lax.fori_loop(0, steps, drain, 0)


def finish(rows_in, maps_in, rows_out, maps_out, rows_held, maps_held, get_sem, put_sem):
    pieces = get_sem.shape[1]
    arrays = ((rows_in, rows_held, rows_out), (maps_in, maps_held, maps_out))

    def move(i, k, sems, put):
        src, held, out = arrays[i]
        count = src.shape[0] // pieces
        rows = pl.ds(k * count, count)
        if put:
            return pltpu.make_async_copy(held.at[rows], out.at[rows], sems.at[i, k])
        return pltpu.make_async_copy(src.at[rows], held.at[rows], sems.at[i, k])

    places = [(i, k) for i in range(2) for k in range(pieces)]
    for i, k in places:
        move(i, k, get_sem, False).start()
    for i, k in places:
        move(i, k, get_sem, False).wait()
        move(i, k, put_sem, True).start()
    for i, k in places:
        move(i, k, put_sem, True).wait()


def per_device(n, tiles, loadings, maps, run_counts):
    frames, _, steps, grays = tiles.shape
    rank = maps.shape[-1]
    lanes, pieces = 128, 4
    chunks = grays // lanes
    half_rows = frames // 2
    piece = half_rows // pieces
    f32, bf16 = jnp.float32, jnp.bfloat16
    anywhere = pl.BlockSpec(memory_space=pl.ANY)
    fetches = 4
    dma = pltpu.SemaphoreType.DMA
    rows_out, maps_out = pl.pallas_call(
        functools.partial(kernel, n, steps),
        out_shape=(
            jax.ShapeDtypeStruct((half_rows, rank), f32),
            jax.ShapeDtypeStruct((grays, rank), f32),
        ),
        in_specs=[anywhere, anywhere, anywhere, pl.BlockSpec(memory_space=pltpu.SMEM)],
        out_specs=(anywhere, anywhere),
        scratch_shapes=[
            pltpu.VMEM((frames * steps, grays), bf16),
            pltpu.VMEM((frames, rank), f32),
            pltpu.VMEM((grays, rank), f32),
            dma((fetches,)),
            dma((fetches,)),
            dma(()),
            dma((pieces,)),
            dma((chunks,)),
            pltpu.VMEM((steps, frames, grays), bf16),
            pltpu.VMEM((frames, lanes), f32),
            pltpu.VMEM((2, frames, rank), bf16),
            pltpu.VMEM((rank, frames), bf16),
            pltpu.VMEM((frames, rank), f32),
            pltpu.VMEM((frames, grays), bf16),
            pltpu.VMEM((rank, grays), bf16),
            pltpu.VMEM((rank, grays), f32),
            pltpu.VMEM((pieces, piece, rank), f32),
            pltpu.VMEM((steps, chunks, rank, lanes), jnp.int16),
            pltpu.VMEM((steps, chunks, rank, lanes), jnp.int16),
            pltpu.VMEM((steps, chunks, 8, lanes), f32),
            pltpu.VMEM((steps, chunks, 8, lanes), f32),
            pltpu.VMEM((2, pieces, piece, rank), bf16),
            pltpu.VMEM((2, pieces, piece, rank), bf16),
            dma((steps, chunks)),
            dma((steps, chunks)),
            dma((steps, chunks)),
            dma((steps, chunks)),
            dma((2, pieces)),
            dma((2, pieces)),
            dma((pieces,)),
            dma((pieces,)),
        ],
        compiler_params=pltpu.CompilerParams(
            collective_id=0, has_side_effects=True, vmem_limit_bytes=56 * 1024 * 1024
        ),
    )(tiles.reshape(frames * steps, grays), loadings, maps[0, 0], run_counts)
    rows_out, maps_out = pl.pallas_call(
        finish,
        out_shape=(
            jax.ShapeDtypeStruct(rows_out.shape, f32),
            jax.ShapeDtypeStruct(maps_out.shape, f32),
        ),
        in_specs=[anywhere, anywhere],
        out_specs=(anywhere, anywhere),
        scratch_shapes=[
            pltpu.VMEM(rows_out.shape, f32),
            pltpu.VMEM(maps_out.shape, f32),
            dma((2, pieces)),
            dma((2, pieces)),
        ],
        compiler_params=pltpu.CompilerParams(vmem_limit_bytes=56 * 1024 * 1024),
    )(rows_out, maps_out)
    return rows_out, maps_out.reshape(maps.shape)


def solution(mesh):
    in_specs = (
        P("blk", "panel", None, None),
        P("blk", None),
        P("blk", "panel", None, None),
        P("blk"),
    )
    out_specs = (P(("blk", "panel"), None), P("blk", "panel", None, None))
    return jax.shard_map(
        functools.partial(per_device, mesh.shape["blk"]),
        mesh=mesh, in_specs=in_specs, out_specs=out_specs, check_vma=False,
    )
```

```python
import functools

import jax
import jax.numpy as jnp
from jax import lax
from jax.experimental import pallas as pl
from jax.experimental.pallas import tpu as pltpu
from jax.sharding import PartitionSpec as P

RUN_LEN = 256
MESH = pl.DeviceIdType.MESH
LEVELS = 32767.0

map_rate = 0.1
load_rate = 0.05


def dot(a, b):
    return jnp.dot(a, b, preferred_element_type=jnp.float32)


def dot_nt(a, b):
    return lax.dot_general(a, b, (((1,), (1,)), ((), ())), preferred_element_type=jnp.float32)


def kernel(
    n, steps, tiles_hbm, loads_hbm, maps_hbm, counts_ref, rows_out, maps_out,
    tiles_ref, loads_ref, maps_ref, tiles_sem, loads_sem, maps_sem, rows_sem, out_sem, data, mask, loads_bf, loads_t, resid, block_t, start_t, cur,
    code_out, code_in, unit_out, unit_in, share_out, share_in,
    code_send, code_recv, unit_send, unit_recv, share_send, share_recv, new_send, new_recv,
):
    frames, rank = loads_ref.shape
    fetches = tiles_sem.shape[0]

    def fetch(src, dst, sems, k):
        count = dst.shape[0] // fetches
        rows = pl.ds(k * count, count)
        return pltpu.make_async_copy(src.at[rows], dst.at[rows], sems.at[k])

    for k in range(fetches):
        fetch(loads_hbm, loads_ref, loads_sem, k).start()
    fetch_maps = pltpu.make_async_copy(maps_hbm, maps_ref, maps_sem)
    fetch_maps.start()

    for k in range(fetches):
        fetch(tiles_hbm, tiles_ref, tiles_sem, k).start()
    grays = maps_ref.shape[0]
    lanes = 128
    chunks = grays // lanes
    half_rows = frames // 2
    half = steps // 2
    scale = 1.0 / rank**0.5
    pieces = share_send.shape[1]
    piece = half_rows // pieces
    me = lax.axis_index("blk")
    panel = lax.axis_index("panel")
    right, left = lax.rem(me + 1, n), lax.rem(me + n - 1, n)
    other = 1 - panel

    barrier = pltpu.get_barrier_semaphore()
    for target in ((left, panel), (right, panel), (me, other)):
        pl.semaphore_signal(barrier, inc=1, device_id=target, device_id_type=MESH)

    def code_copy(step, c):
        return pltpu.make_async_remote_copy(
            src_ref=code_out.at[step, c], dst_ref=code_in.at[step, c],
            send_sem=code_send.at[step, c], recv_sem=code_recv.at[step, c],
            device_id=(right, panel), device_id_type=MESH)

    def unit_copy(step, c):
        return pltpu.make_async_remote_copy(
            src_ref=unit_out.at[step, c], dst_ref=unit_in.at[step, c],
            send_sem=unit_send.at[step, c], recv_sem=unit_recv.at[step, c],
            device_id=(right, panel), device_id_type=MESH)

    def share_copy(part, k):
        return pltpu.make_async_remote_copy(
            src_ref=share_out.at[part, k], dst_ref=share_in.at[part, k],
            send_sem=share_send.at[part, k], recv_sem=share_recv.at[part, k],
            device_id=(me, other), device_id_type=MESH)

    def rows_of(owner, k):
        return pl.ds(pl.multiple_of(owner * half_rows + k * piece, piece), piece)

    def new_copy(owner, k):
        rows = rows_of(owner, k)
        return pltpu.make_async_remote_copy(
            src_ref=loads_bf.at[1, rows], dst_ref=loads_bf.at[1, rows],
            send_sem=new_send.at[k], recv_sem=new_recv.at[k],
            device_id=(me, other), device_id_type=MESH)

    for r in range(0, frames, RUN_LEN):
        if r % (frames // fetches) == 0:
            fetch(loads_hbm, loads_ref, loads_sem, r // (frames // fetches)).wait()
        part_bf = loads_ref[r : r + RUN_LEN, :].astype(jnp.bfloat16)
        loads_bf[0, r : r + RUN_LEN, :] = part_bf
        loads_t[:, r : r + RUN_LEN] = part_bf.T
        within = lax.broadcasted_iota(jnp.int32, (RUN_LEN, lanes), 0)
        mask[r : r + RUN_LEN, :] = (within < counts_ref[r // RUN_LEN]).astype(jnp.float32)
    fetch_maps.wait()
    start_t[...] = maps_ref[...].T

    group = 256
    each = group // steps
    to = lax.broadcasted_iota(jnp.int32, (group, group), 0)
    frm = lax.broadcasted_iota(jnp.int32, (group, group), 1)
    order = jnp.where(frm == lax.rem(to, each) * steps + to // each, 1.0, 0.0).astype(jnp.bfloat16)

    blocks = frames * steps // group
    per_fetch = blocks // fetches

    def sort_steps(first, stop, per_turn):
        def turn(i, carry):
            for j in range(per_turn):
                at = i * per_turn + j
                block = tiles_ref[pl.ds(pl.multiple_of(at * group, group), group), :]
                sorted_rows = dot(order[first * each : stop * each, :], block).astype(jnp.bfloat16)
                for s in range(first, stop):
                    data[s, pl.ds(pl.multiple_of(at * each, each), each), :] = (
                        sorted_rows[(s - first) * each : (s - first + 1) * each, :])
            return carry

        return turn

    for k in range(fetches):
        fetch(tiles_hbm, tiles_ref, tiles_sem, k).wait()
        sort_steps(0, 1, per_fetch)(k, 0)
    pl.semaphore_wait(barrier, 3)

    def decoded(step, c):
        return code_in[step, c].astype(jnp.float32) * unit_in[step, c][0:1, :]

    def send_block(step, c, new):
        top = jnp.maximum(jnp.max(jnp.abs(new), axis=0, keepdims=True), 1e-30)
        code_out[step, c] = jnp.round(new * (LEVELS / top)).astype(jnp.int32).astype(jnp.int16)
        unit_out[step, c] = jnp.broadcast_to(top * (1.0 / LEVELS), (8, lanes))
        unit_copy(step, c).start()
        code_copy(step, c).start()

    def run_step(step, part, first=False):
        for c in range(chunks):
            cols = slice(c * lanes, (c + 1) * lanes)
            if first:
                held = start_t[:, cols]
            else:
                code_copy(step - 1, c).wait_recv()
                unit_copy(step - 1, c).wait_recv()
                held = decoded(step - 1, c)
            block = held.astype(jnp.bfloat16)
            block_t[step, :, cols] = block
            for r in range(0, frames, RUN_LEN):
                rows = slice(r, r + RUN_LEN)
                prod = dot(loads_bf[part, rows, :], block)
                tile = data[step, rows, cols].astype(jnp.float32)
                resid[step, rows, cols] = ((tile - prod * scale) * mask[rows, :]).astype(jnp.bfloat16)
            new = held + (map_rate * scale) * dot(loads_t[...], resid[step, :, cols])
            send_block(step, c, new)

    def half_sum(part, rows):
        total = dot_nt(resid[part * half, rows, :], block_t[part * half])
        for step in range(part * half + 1, (part + 1) * half):
            total = total + dot_nt(resid[step, rows, :], block_t[step])
        return total

    def share_copies(part):
        for k in range(pieces):
            share_out[part, k] = half_sum(part, rows_of(other, k)).astype(jnp.bfloat16)
            share_copy(part, k).start()

    def write_maps(c):
        rows = pl.ds(c * lanes, lanes)
        return pltpu.make_async_copy(maps_ref.at[rows], maps_out.at[rows], out_sem.at[c])

    def write_rows(k):
        return pltpu.make_async_copy(cur.at[k], rows_out.at[pl.ds(k * piece, piece)], rows_sem.at[k])

    def total_of(part, k):
        total = half_sum(part, rows_of(panel, k))
        share_copy(part, k).wait_recv()
        total = total + share_in[part, k].astype(jnp.float32)
        return total * (load_rate * scale)

    run_step(0, 0, first=True)
    lax.fori_loop(0, 2 * fetches, sort_steps(1, steps, per_fetch // 2), 0)

    def first_half(step, carry):
        run_step(step, 0)
        return carry

    lax.fori_loop(1, half, first_half, 0)
    share_copies(0)

    for c in range(chunks):
        cols = slice(c * lanes, (c + 1) * lanes)
        code_copy(half - 1, c).wait_recv()
        unit_copy(half - 1, c).wait_recv()
        held = decoded(half - 1, c)
        start_t[:, cols] = held
        block_t[half, :, cols] = held.astype(jnp.bfloat16)

    def run_piece(rows):
        rows_bf = loads_bf[1, rows, :]
        rows_t = rows_bf.T
        loads_t[:, rows] = rows_t
        prod = dot(rows_bf, block_t[half])
        for c in range(chunks):
            cols = slice(c * lanes, (c + 1) * lanes)
            tile = data[half, rows, cols].astype(jnp.float32)
            resid[half, rows, cols] = ((tile - prod[:, cols] * scale) * mask[rows, :]).astype(jnp.bfloat16)
        part_resid = resid[half, rows, :]
        start_t[...] += (map_rate * scale) * dot(rows_t, part_resid)

    for k in range(pieces):
        rows = rows_of(panel, k)
        own = loads_ref[rows, :] + total_of(0, k)
        cur[k] = own
        loads_bf[1, rows, :] = own.astype(jnp.bfloat16)
        new_copy(panel, k).start()
        run_piece(rows)
    for k in range(pieces):
        new_copy(other, k).wait_recv()
        run_piece(rows_of(other, k))
    for c in range(chunks):
        send_block(half, c, start_t[:, c * lanes : (c + 1) * lanes])

    def second_half(step, carry):
        run_step(step, 1)
        return carry

    lax.fori_loop(half + 1, steps, second_half, 0)
    share_copies(1)

    for k in range(pieces):
        if k == pieces - 1:
            for c in range(chunks):
                code_copy(steps - 1, c).wait_recv()
                unit_copy(steps - 1, c).wait_recv()
                maps_ref[c * lanes : (c + 1) * lanes, :] = decoded(steps - 1, c).T
                write_maps(c).start()
        cur[k] = cur[k] + total_of(1, k)
        write_rows(k).start()
    for c in range(chunks):
        write_maps(c).wait()
    for k in range(pieces):
        write_rows(k).wait()

    for k in range(pieces):
        new_copy(panel, k).wait_send()
        for part in range(2):
            share_copy(part, k).wait_send()

    def drain(step, carry):
        for c in range(chunks):
            code_copy(step, c).wait_send()
            unit_copy(step, c).wait_send()
        return carry

    lax.fori_loop(0, steps, drain, 0)


def finish(rows_in, maps_in, rows_out, maps_out, rows_held, maps_held, get_sem, put_sem):
    pieces = get_sem.shape[1]
    arrays = ((rows_in, rows_held, rows_out), (maps_in, maps_held, maps_out))

    def move(i, k, sems, put):
        src, held, out = arrays[i]
        count = src.shape[0] // pieces
        rows = pl.ds(k * count, count)
        if put:
            return pltpu.make_async_copy(held.at[rows], out.at[rows], sems.at[i, k])
        return pltpu.make_async_copy(src.at[rows], held.at[rows], sems.at[i, k])

    places = [(i, k) for i in range(2) for k in range(pieces)]
    for i, k in places:
        move(i, k, get_sem, False).start()
    for i, k in places:
        move(i, k, get_sem, False).wait()
        move(i, k, put_sem, True).start()
    for i, k in places:
        move(i, k, put_sem, True).wait()


def per_device(n, tiles, loadings, maps, run_counts):
    frames, _, steps, grays = tiles.shape
    rank = maps.shape[-1]
    lanes, pieces = 128, 4
    chunks = grays // lanes
    half_rows = frames // 2
    piece = half_rows // pieces
    f32, bf16 = jnp.float32, jnp.bfloat16
    anywhere = pl.BlockSpec(memory_space=pl.ANY)
    fetches = 4
    dma = pltpu.SemaphoreType.DMA
    rows_out, maps_out = pl.pallas_call(
        functools.partial(kernel, n, steps),
        out_shape=(
            jax.ShapeDtypeStruct((half_rows, rank), f32),
            jax.ShapeDtypeStruct((grays, rank), f32),
        ),
        in_specs=[anywhere, anywhere, anywhere, pl.BlockSpec(memory_space=pltpu.SMEM)],
        out_specs=(anywhere, anywhere),
        scratch_shapes=[
            pltpu.VMEM((frames * steps, grays), bf16),
            pltpu.VMEM((frames, rank), f32),
            pltpu.VMEM((grays, rank), f32),
            dma((fetches,)),
            dma((fetches,)),
            dma(()),
            dma((pieces,)),
            dma((chunks,)),
            pltpu.VMEM((steps, frames, grays), bf16),
            pltpu.VMEM((frames, lanes), f32),
            pltpu.VMEM((2, frames, rank), bf16),
            pltpu.VMEM((rank, frames), bf16),
            pltpu.VMEM((steps, frames, grays), bf16),
            pltpu.VMEM((steps, rank, grays), bf16),
            pltpu.VMEM((rank, grays), f32),
            pltpu.VMEM((pieces, piece, rank), f32),
            pltpu.VMEM((steps, chunks, rank, lanes), jnp.int16),
            pltpu.VMEM((steps, chunks, rank, lanes), jnp.int16),
            pltpu.VMEM((steps, chunks, 8, lanes), f32),
            pltpu.VMEM((steps, chunks, 8, lanes), f32),
            pltpu.VMEM((2, pieces, piece, rank), bf16),
            pltpu.VMEM((2, pieces, piece, rank), bf16),
            dma((steps, chunks)),
            dma((steps, chunks)),
            dma((steps, chunks)),
            dma((steps, chunks)),
            dma((2, pieces)),
            dma((2, pieces)),
            dma((pieces,)),
            dma((pieces,)),
        ],
        compiler_params=pltpu.CompilerParams(
            collective_id=0, has_side_effects=True, vmem_limit_bytes=56 * 1024 * 1024
        ),
    )(tiles.reshape(frames * steps, grays), loadings, maps[0, 0], run_counts)
    rows_out, maps_out = pl.pallas_call(
        finish,
        out_shape=(
            jax.ShapeDtypeStruct(rows_out.shape, f32),
            jax.ShapeDtypeStruct(maps_out.shape, f32),
        ),
        in_specs=[anywhere, anywhere],
        out_specs=(anywhere, anywhere),
        scratch_shapes=[
            pltpu.VMEM(rows_out.shape, f32),
            pltpu.VMEM(maps_out.shape, f32),
            dma((2, pieces)),
            dma((2, pieces)),
        ],
        compiler_params=pltpu.CompilerParams(vmem_limit_bytes=56 * 1024 * 1024),
    )(rows_out, maps_out)
    return rows_out, maps_out.reshape(maps.shape)


def solution(mesh):
    in_specs = (
        P("blk", "panel", None, None),
        P("blk", None),
        P("blk", "panel", None, None),
        P("blk"),
    )
    out_specs = (P(("blk", "panel"), None), P("blk", "panel", None, None))
    return jax.shard_map(
        functools.partial(per_device, mesh.shape["blk"]),
        mesh=mesh, in_specs=in_specs, out_specs=out_specs, check_vma=False,
    )
```
